32 devices in a mesh: gx: 8 (over y, x, core), wa: 4 (over z).
Axes of the slice: x: 2, y: 2, z: 4, core: 2. Of those that a mesh axis runs over, the one named last changes fastest.
Arguments:
- les_flow: bfloat16 [4, 512, 32, 256], P(None, 'gx', None, 'wa'), may hold values from -2.5 to 2.5
- y_index: int32 [128], replicated, may hold values from 0 to 254
- y_weight: bfloat16 [128], replicated, may hold values from 0 to 1
- acoustic_state: float32 [4, 1024, 64, 128], P(None, 'gx', 'wa'), may hold values from -6 to 6
Outputs:
- advanced_state: float32 [4, 1024, 64, 128], P(None, 'gx', 'wa')
The draws below stay inside these ranges and needn't reach their ends.
All inputs are finite; a program needn't handle non-finite values.
Results may differ from the reference program's by a relative error of at most 0.0014.
Values may be sent and summed in bfloat16 or wider, within the bound.
No kernel may reach another device: no remote copies, remote signals or barrier semaphores. Data moves between devices by JAX's collectives and lax.ppermute only.
A program may use at most 128 MiB of HBM per device.

```python
import jax
import jax.numpy as jnp
from jax import lax

AY = 128
LX = 512
AX = 1024
LY = 256
AZ = 64
LZ = 32


def with_ends(array, rng, low, high):
    longest = array.shape.index(max(array.shape))
    spots = []
    for shift in (0, 1):
        where = [jax.random.randint(jax.random.fold_in(rng, axis), (), 0, length) for axis, length in enumerate(array.shape)]
        where[longest] = (where[longest] + shift) % array.shape[longest]
        spots.append(tuple(where))
    return array.at[spots[0]].set(low).at[spots[1]].set(high)


def shard_levels(own_key, shape, pieces, low, high):
    factor_of, own = 1.0, jax.random.fold_in(own_key, 6)
    for position, shards_of in pieces:
        steps = jnp.exp(jax.random.uniform(jax.random.fold_in(own, position), (shards_of,), jnp.float32, low / len(pieces), high / len(pieces)))
        factor_of = factor_of * jnp.repeat(steps, shape[position] // shards_of).reshape([-1 if axis == position else 1 for axis in range(len(shape))])
    return factor_of


def bell_draw(own_key, shape, deviation, reach, shards=(), held_as=jnp.bfloat16):
    loudness = shard_levels(own_key, shape, shards, -0.22, 0.18) if shards else 1.0
    entries = jax.random.normal(own_key, shape, jnp.float32) * deviation * loudness
    return jnp.minimum(jnp.maximum(entries, -reach), reach).astype(held_as)


def setup_inputs(seed: int = 0) -> dict:
    keys = jax.random.split(jax.random.key(seed), 5)
    les_flow = bell_draw(keys[0], (4, LX, LZ, LY), 1.0, 2.5, ((1, 8), (3, 4)))
    y_index = with_ends(jax.random.randint(keys[1], (AY,), 0, LY - 1), jax.random.fold_in(keys[1], 1), 0, (LY - 1) - 1).astype(jnp.int32)
    y_weight = jnp.clip(jax.random.uniform(keys[2], (AY,), jnp.float32, 0.0, 1.0), 0.0, 1.0).astype(jnp.bfloat16)
    acoustic_state = bell_draw(keys[3], (4, AX, AZ, AY), 1.0, 6.0, ((1, 8), (2, 4)), jnp.float32)
    return {"les_flow": les_flow, "y_index": y_index, "y_weight": y_weight, "acoustic_state": acoustic_state}


time_step = 0.4


def refine(coarse, which_axis, following):
    length = coarse.shape[which_axis]
    after = jnp.concatenate([lax.slice_in_dim(coarse, 1, length, axis=which_axis), following], axis=which_axis)
    midpoint = 0.5 * (coarse + after)
    stacked = jnp.stack([coarse, midpoint], axis=which_axis + 1)
    new_shape = list(coarse.shape)
    new_shape[which_axis] = 2 * length
    return stacked.reshape(new_shape)


def central(padded, which_axis, length):
    def offset_slice(offset):
        return lax.slice_in_dim(padded, offset, offset + length, axis=which_axis)
    return (8.0 * (offset_slice(3) - offset_slice(1)) - (offset_slice(4) - offset_slice(0))) / 12.0


def tendency(fields, coeffs, along_x, along_z):
    along_y = jnp.pad(fields, ((0, 0), (0, 0), (0, 0), (2, 2)))
    slope_x = central(along_x, 1, fields.shape[1])
    slope_z = central(along_z, 2, fields.shape[2])
    slope_y = central(along_y, 3, fields.shape[3])
    speed_x = 0.3 * coeffs[0]
    speed_y = 0.3 * coeffs[1]
    speed_z = 0.3 * coeffs[2]
    sound_speed = 1.0 + 0.2 * coeffs[3]
    carried = speed_x * slope_x + speed_y * slope_y + speed_z * slope_z
    spread = slope_x[1] + slope_y[2] + slope_z[3]
    return jnp.stack([
        -carried[0] - sound_speed * sound_speed * spread,
        -carried[1] - slope_x[0],
        -carried[2] - slope_y[0],
        -carried[3] - slope_z[0]])


def full_rate(fields, coeffs):
    padded = jnp.pad(fields, ((0, 0), (2, 2), (2, 2), (0, 0)))
    return tendency(fields, coeffs, padded[:, :, 2:-2], padded[:, 2:-2])


def reference(les_flow, y_index, y_weight, acoustic_state):
    left_weight = lax.optimization_barrier((1.0 - y_weight.astype(jnp.float32)).astype(jnp.bfloat16)).astype(jnp.float32)
    right_weight = y_weight.astype(jnp.float32)
    lower = jnp.take(les_flow, y_index, axis=3).astype(jnp.float32)
    upper = jnp.take(les_flow, y_index + 1, axis=3).astype(jnp.float32)
    spanwise = lower * left_weight + upper * right_weight
    fine_z = refine(spanwise, 2, spanwise[:, :, -1:, :])
    coeffs = refine(fine_z, 1, fine_z[:, -1:])
    rate_one = full_rate(acoustic_state, coeffs)
    rate_two = full_rate(acoustic_state + 0.5 * time_step * rate_one, coeffs)
    rate_three = full_rate(acoustic_state + 0.5 * time_step * rate_two, coeffs)
    rate_four = full_rate(acoustic_state + time_step * rate_three, coeffs)
    return acoustic_state + (time_step / 6.0) * (rate_one + 2.0 * rate_two + 2.0 * rate_three + rate_four)
```

```python
import functools

import jax
import jax.numpy as jnp
from jax import lax
from jax.experimental import pallas as pl
from jax.experimental.pallas import tpu as pltpu
from jax.sharding import PartitionSpec as P

time_step = 0.4
unit = time_step / 12.0
reach = 8
ahead = 4
layers = 4
pad = 8
group = 3
f32 = jnp.float32
bf16 = jnp.bfloat16
grant = 60 * 2**20
vmem = pl.BlockSpec(memory_space=pltpu.VMEM)
hbm = pl.BlockSpec(memory_space=pl.ANY)


def shape_of(*dims, dtype=f32):
    return jax.ShapeDtypeStruct(dims, dtype)


def call(kernel, out_shape, in_specs, out_specs, scratch=()):
    return pl.pallas_call(
        kernel,
        out_shape=out_shape,
        in_specs=in_specs,
        out_specs=out_specs,
        scratch_shapes=list(scratch),
        compiler_params=pltpu.CompilerParams(vmem_limit_bytes=grant),
    )


def edge(axis):
    me = lax.axis_index(axis)
    return (me == 0, me == lax.axis_size(axis) - 1)


def up(value):
    return pltpu.roll(value, 1, 0)


def down(value):
    return pltpu.roll(value, 7, 0)


def side_by_side(les, pair, column):
    return jnp.concatenate(
        [les[2 * pair, column].astype(f32), les[2 * pair + 1, column].astype(f32)], axis=1
    )


def cut_kernel(les, state, *refs):
    *tiles, first, last, wide, ends, sem = refs
    devices = len(tiles)
    columns, levels, width = les.shape[1:]
    own = levels // devices
    me = lax.axis_index("wa")
    starts = (0, state.shape[1] - reach)
    copies = [
        pltpu.make_async_copy(state.at[:, pl.ds(starts[end], reach)], ends.at[end], sem.at[end])
        for end in range(2)
    ]
    for copy in copies:
        copy.start()

    def body(column, carry):
        for pair in range(2):
            wide[pair, column] = jnp.concatenate(
                [les[2 * pair, column].astype(f32), les[2 * pair + 1, column].astype(f32)], axis=1
            )
        return carry

    lax.fori_loop(0, columns, body, 0, unroll=8)
    for shift in range(devices):
        row = pl.multiple_of(lax.rem(me + shift, devices) * own, own)
        tiles[shift][...] = (
            wide[:, :, pl.ds(row, own), :].reshape(2 * columns * own, 2 * width).astype(bf16)
        )
    rows = 4 * reach * state.shape[2]
    les_rows = 2 * ahead * levels
    for end, (target, start) in enumerate(((first, 0), (last, columns - ahead))):
        copies[end].wait()
        target[pl.ds(0, rows), :] = ends[end].reshape(rows, 128).astype(bf16)
        target[pl.ds(rows, les_rows), :] = (
            wide[:, start : start + ahead].reshape(les_rows, 128).astype(bf16)
        )


def cut_tiles(les_flow, state, devices):
    _, columns, levels, width = les_flow.shape
    tile = shape_of(2 * columns * (levels // devices), 2 * width, dtype=bf16)
    end = shape_of(4 * reach * state.shape[2] + 2 * ahead * levels, 128, dtype=bf16)
    *tiles, first, last = call(
        cut_kernel,
        [tile] * devices + [end] * 2,
        [vmem, hbm],
        [vmem] * (devices + 2),
        [
            pltpu.VMEM((2, columns, levels, 2 * width), f32),
            pltpu.VMEM((2, 4, reach, state.shape[2], 128), f32),
            pltpu.SemaphoreType.DMA((2,)),
        ],
    )(les_flow, state)
    return (tiles, first, last)


def tails_kernel(skip, levels, before, after, *refs):
    tails, wide = (refs[:-1], refs[-1])
    devices = len(tails)
    own = levels // devices
    rows = 2 * ahead * levels
    wide[0] = before[pl.ds(skip, rows), :].astype(f32).reshape(2, ahead, levels, 128)
    wide[1] = after[pl.ds(skip, rows), :].astype(f32).reshape(2, ahead, levels, 128)
    me = lax.axis_index("wa")
    for shift in range(devices):
        row = pl.multiple_of(lax.rem(me + shift, devices) * own, own)
        tails[shift][...] = (
            wide[:, :, :, pl.ds(row, own), :].reshape(4 * ahead * own, 128).astype(bf16)
        )


def cut_tails(before, after, skip, levels, devices):
    tail = shape_of(4 * ahead * (levels // devices), 128, dtype=bf16)
    return call(
        functools.partial(tails_kernel, skip, levels),
        [tail] * devices,
        [vmem, vmem],
        [vmem] * devices,
        [pltpu.VMEM((2, 2, ahead, levels, 128), f32)],
    )(before, after)


def run_rows(s, run, height):
    first = max(0, reach - run * s)
    count = min(run, 8 * run - reach - run * s) - first
    inner = pl.ds(first * height, count * height)
    return (inner, pl.ds((run * s + first - reach) * height, count * height))


def widen_kernel(state, before, after, out, send_low, send_high, whole, result, sem, out_sem):
    height, run = out.shape[1:3]
    pitch = run * height + pad
    flat_whole = whole.reshape(32 * pitch, 128)
    fetches = []
    for f in range(4):
        for s in range(8):
            inner, outer = run_rows(s, run, height)
            fetches.append(
                pltpu.make_async_copy(state.at[f, outer], whole.at[f, s, inner], sem.at[f, s])
            )
    for fetch in fetches:
        fetch.start()
    rows = reach * height
    for f in range(4):
        part = pl.ds(f * rows, rows)
        whole[f, 0, pl.ds(0, rows), :] = before[part, :].astype(f32)
        whole[f, 7, pl.ds(run * height - rows, rows), :] = after[part, :].astype(f32)
    pushes = []
    for f in range(4):
        for s in range(8):
            fetches[8 * f + s].wait()

        def body(step, carry, f=f):
            for p in range(4):
                for i in range(run):
                    start = f * 8 * pitch + i * height + 4 * step + p
                    result[f, 4 * step + p, i] = flat_whole[pl.ds(start, 8, stride=pitch), :]
            return carry

        lax.fori_loop(0, height // 4, body, 0)
        push = pltpu.make_async_copy(result.at[f], out.at[f], out_sem.at[f])
        push.start()
        pushes.append(push)
    cast_layers(result, send_low, send_high)
    for push in pushes:
        push.wait()


def cast_layers(result, send_low, send_high):
    _, height, run = result.shape[:3]
    rows = run * 8
    for f in range(4):
        for z in range(layers):
            at = pl.ds((f * layers + z) * rows, rows)
            send_low[at, :] = result[f, z].reshape(rows, 128).astype(bf16)
            send_high[at, :] = result[f, height - layers + z].reshape(rows, 128).astype(bf16)


def widen(state, before, after):
    columns, height = state.shape[1:3]
    run = (columns + 2 * reach) // 8
    layer = shape_of(4 * layers * run * 8, 128, dtype=bf16)
    return call(
        widen_kernel,
        [shape_of(4, height, run, 8, 128), layer, layer],
        [hbm, vmem, vmem],
        [hbm, vmem, vmem],
        [
            pltpu.VMEM((4, 8, run * height + pad, 128), f32),
            pltpu.VMEM((4, height, run, 8, 128), f32),
            pltpu.SemaphoreType.DMA((4, 8)),
            pltpu.SemaphoreType.DMA((4,)),
        ],
    )(state.reshape(4, columns * height, 128), before, after)


def spread_kernel(devices, width, *refs):
    tiles, tails = (refs[:devices], refs[devices : 2 * devices])
    y_index, y_weight, out, send_low, send_high, wide = refs[2 * devices :]
    me = lax.axis_index("wa")
    left_weight = (1.0 - y_weight[...].astype(f32)).astype(bf16).astype(f32)
    right_weight = y_weight[...].astype(f32)
    row_ids = lax.broadcasted_iota(jnp.int32, (width, 128), 0)
    nothing = jnp.zeros((width, 128), f32)
    total, tail = (None, None)
    for shift in range(devices):
        first_row = lax.rem(me - shift + devices, devices) * width
        gap = y_index[...] - first_row - row_ids
        matrix = jnp.where(gap == 0, left_weight, 0.0) + jnp.where(gap == -1, right_weight, 0.0)
        pair = jnp.concatenate(
            [
                jnp.concatenate([matrix, nothing], axis=1),
                jnp.concatenate([nothing, matrix], axis=1),
            ],
            axis=0,
        ).astype(bf16)
        part = jnp.dot(tiles[shift][...], pair, preferred_element_type=f32)
        tail_part = jnp.dot(tails[shift][...], pair, preferred_element_type=f32)
        total = part if total is None else total + part
        tail = tail_part if tail is None else tail + tail_part
    levels, run = (out.shape[1], out.shape[2] - 1)
    columns = total.shape[0] // (2 * levels)
    wide_columns = columns + 2 * ahead
    _, is_end = edge("gx")
    for f in range(4):
        pair, lanes = (f // 2, slice(128 * (f % 2), 128 * (f % 2 + 1)))
        main = total[pair * columns * levels : (pair + 1) * columns * levels, lanes]
        side = ahead * levels
        left = tail[pair * side : (pair + 1) * side, lanes]
        right = tail[(2 + pair) * side : (3 + pair) * side, lanes]
        right = jnp.where(is_end, jnp.concatenate([main[-levels:]] * ahead, axis=0), right)
        wide[pl.ds(f * wide_columns * levels, wide_columns * levels), :] = jnp.concatenate(
            [left, main, right], axis=0
        )
    for f in range(4):

        def body(k, carry, f=f):
            for j in range(run):
                start = (f * wide_columns + j) * levels + k
                value = wide[pl.ds(start, 8, stride=run * levels), :]
                out[f, k, j] = value
                if j == 0:
                    out[f, k, run] = down(value)
            return carry

        lax.fori_loop(0, levels, body, 0)
        rows = run * 8
        at = pl.ds(f * rows, rows)
        send_high[at, :] = out[f, levels - 1, :run].reshape(rows, 128).astype(bf16)
        for k in range(2):
            send_low[k, at, :] = out[f, k, :run].reshape(rows, 128).astype(bf16)


def spread(tiles, tails, y_index, y_weight, columns, levels, width):
    devices = len(tiles)
    run = (columns + 2 * ahead) // 8
    return call(
        functools.partial(spread_kernel, devices, width),
        [
            shape_of(4, levels, run + 1, 8, 128),
            shape_of(2, 4 * run * 8, 128, dtype=bf16),
            shape_of(4 * run * 8, 128, dtype=bf16),
        ],
        [vmem] * (2 * devices + 2),
        [vmem] * 3,
        [pltpu.VMEM((4 * (columns + 2 * ahead) * levels, 128), f32)],
    )(*tiles, *tails, y_index.reshape(1, 128), y_weight.reshape(1, 128))


def band_matrix():
    row, column = [lax.broadcasted_iota(jnp.int32, (256, 256), axis) for axis in range(2)]
    gap = jnp.where((row < 128) == (column < 128), row - column, 128)
    near = jnp.where(gap == 1, 8.0, jnp.where(gap == -1, -8.0, 0.0))
    return (near + jnp.where(gap == 2, -1.0, jnp.where(gap == -2, 1.0, 0.0))).astype(bf16)


def difference(low_far, low, high, high_far):
    return 8.0 * (high - low) - (high_far - low_far)


def spanwise(source, plane, slopes, band):
    run = source.shape[2] - 4
    for pair in range(2):
        sides = [
            source[f, pl.ds(plane, 2), pl.ds(2, run)].reshape(2 * run * 8, 128).astype(bf16)
            for f in (2 * pair, 2 * pair + 1)
        ]
        both = jnp.dot(jnp.concatenate(sides, axis=1), band, preferred_element_type=f32)
        slopes[2 * pair] = both[:, :128].reshape(2, run, 8, 128)
        slopes[2 * pair + 1] = both[:, 128:].reshape(2, run, 8, 128)


def stage(source, plane, coeffs, across, anchor, store, slopes_y, factor):
    run = coeffs.shape[2]
    places = [(p, u) for p in range(2) for u in range(group)]
    for first in range(0, run, group):
        speeds = {
            (f, p, u): coeffs[f, across + p, first + u] for f in range(3) for p, u in places
        }
        rates, spreads, own_rates, centers = ({}, {}, {}, {})
        for f in range(4):
            line = {
                (p, u): source[f, plane + p, first + u + 2]
                for p in range(2)
                for u in range(-2, group + 2)
            }
            for u in range(group):
                for p in (-2, -1, 2, 3):
                    line[p, u] = source[f, plane + p, first + u + 2]
            for p, u in places:
                slope_x = difference(*[line[p, u + k] for k in (-2, -1, 1, 2)])
                slope_z = difference(*[line[p + k, u] for k in (-2, -1, 1, 2)])
                slope_y = slopes_y[f, p, first + u]
                rate = (
                    speeds[0, p, u] * slope_x + speeds[1, p, u] * slope_y + speeds[2, p, u] * slope_z
                )
                if f == 0:
                    own_rates[p, u] = rate
                    centers[p, u] = line[p, u]
                    for k, slope in enumerate((slope_x, slope_y, slope_z)):
                        rates[k + 1, p, u] = unit * slope
                else:
                    rate += rates[f, p, u]
                    start = line[p, u] if anchor is None else anchor(f, p, first + u)
                    store(f, p, first + u, start - factor * rate)
                    slope = (slope_x, slope_y, slope_z)[f - 1]
                    spreads[p, u] = slope if f == 1 else spreads[p, u] + slope
        for p, u in places:
            rate = own_rates[p, u] + coeffs[3, across + p, first + u] * spreads[p, u]
            start = centers[p, u] if anchor is None else anchor(0, p, first + u)
            store(0, p, first + u, start - factor * rate)


def fill_coeffs(flow, level, coeffs, plane):
    run = coeffs.shape[2]
    for f in range(4):
        here = [flow[f, level, j] for j in range(run // 2 + 1)]
        above = [flow[f, level + 1, j] for j in range(run // 2 + 1)]
        middle = [0.5 * (a + b) for a, b in zip(here, above)]
        for p, line in enumerate((here, middle)):
            for i in range(run):
                j = i // 2
                value = line[j] if i % 2 == 0 else 0.5 * (line[j] + line[j + 1])
                if f < 3:
                    value = (0.3 * unit) * value
                else:
                    speed = 1.0 + 0.2 * value
                    value = unit * (speed * speed)
                coeffs[f, plane + p, i] = value


def put_plane(target, f, plane, values):
    run = len(values)
    for i, value in enumerate(values):
        target[f, plane, i + 2] = value
    for i in range(2):
        target[f, plane, i] = up(values[run - 2 + i])
        target[f, plane, run + 2 + i] = down(values[i])


def close_planes(target, plane):
    run = target.shape[2] - 4
    for f in range(4):
        for i in range(2):
            target[f, plane, i] = up(target[f, plane, run + i])
            target[f, plane, run + 2 + i] = down(target[f, plane, 2 + i])


def mask_columns(target, planes, offset, left, right):
    run = target.shape[2] - 2 * offset
    sublane = lax.broadcasted_iota(jnp.int32, (8, 128), 0)

    @pl.when(left)
    def _():
        for f in range(4):
            for plane in planes:
                for i in range(reach):
                    value = target[f, plane, offset + i]
                    target[f, plane, offset + i] = jnp.where(sublane == 0, 0.0, value)

    @pl.when(right)
    def _():
        for f in range(4):
            for plane in planes:
                for i in range(run - reach, run):
                    value = target[f, plane, offset + i]
                    target[f, plane, offset + i] = jnp.where(sublane == 7, 0.0, value)


class Sweep:
    def __init__(self, fields, middle, coeffs, slopes, flow, result, base, factors, shift):
        self.fields, self.middle, self.coeffs, self.slopes = (fields, middle, coeffs, slopes)
        self.flow, self.result, self.base, self.factors = (flow, result, base, factors)
        self.shift = shift
        self.run = coeffs.shape[2]
        self.band = band_matrix()
        self.left, self.right = edge("gx")

    def fill(self, step):
        fill_coeffs(self.flow, step, self.coeffs, 2 * step)

    def first_slopes(self, step, slot=0):
        spanwise(self.fields, 2 * step + 2, self.slopes.at[slot], self.band)

    def first(self, step, slot=0):
        run, middle, base = (self.run, self.middle, self.base)

        def store(f, p, i, value):
            plane = 2 * step + p
            middle[f, plane, i + 2] = value
            if i < 2:
                middle[f, plane, run + 2 + i] = down(value)
            if i >= run - 2:
                middle[f, plane, i - (run - 2)] = up(value)

        anchor = None
        if base is not None:

            def anchor(f, p, i):
                return base[f, 2 * step + p, i]

        stage(
            self.fields, 2 * step + 2, self.coeffs, 2 * step, anchor, store,
            self.slopes.at[slot], self.factors[0],
        )

    def mask_first(self, step):
        mask_columns(self.middle, [2 * step, 2 * step + 1], 2, self.left, self.right)

    def clear_first(self, step):
        for f in range(4):
            for p in range(2):
                for i in range(self.run + 4):
                    self.middle[f, 2 * step + p, i] = jnp.zeros((8, 128), f32)

    def last_slopes(self, step, slot=2):
        spanwise(self.middle, 2 * step + 2, self.slopes.at[slot], self.band)

    def last(self, step, slot=2):
        run, result = (self.run, self.result)

        def anchor(f, p, i):
            if self.base is not None:
                return self.base[f, 2 * step + 2 + p, i]
            return self.fields[f, 2 * step + 4 + p, i + 2]

        def store(f, p, i, value):
            z = 2 * step + p
            if self.base is None:
                result[f, z - self.shift(step), i] = value
            else:
                pitch = result.shape[2]
                height = (pitch - pad) // run
                flat_result = result.reshape(32 * pitch, 128)
                flat_result[pl.ds(f * 8 * pitch + i * height + z, 8, stride=pitch), :] = value

        stage(
            self.middle, 2 * step + 2, self.coeffs, 2 * step + 2, anchor, store,
            self.slopes.at[slot], self.factors[1],
        )

    def mask_last(self, step):
        if self.base is None:
            first = 2 * step - self.shift(step)
            mask_columns(self.result, [first, first + 1], 0, self.left, self.right)


def inner_kernel(factors, final, *refs):
    if final:
        inner, outer, flow_in, anchor, out, edges = refs[:6]
        scratch = refs[6:]
        base, q_sem = scratch[-2:]
    else:
        state, flow_in, out, edges = refs[:4]
        scratch = refs[4:]
        base = None
    fields, middle, coeffs, result, slopes, flow, in_sem, out_sem, flow_sem = scratch[:9]
    run = coeffs.shape[2]
    levels = flow_in.shape[1]
    pairs = in_sem.shape[0]

    def source(pair):
        if not final:
            return state.at[:, pl.ds(2 * pair, 2)]
        if pair < 2:
            return outer.at[:, pl.ds(2 * pair, 2)]
        if pair >= pairs - 2:
            return outer.at[:, pl.ds(2 * (pair - (pairs - 4)), 2)]
        return inner.at[:, pl.ds(2 * (pair - 2), 2)]

    flow_copy = pltpu.make_async_copy(flow_in, flow.at[:, pl.ds(1, levels)], flow_sem)
    flow_copy.start()
    copies = []
    for pair in range(pairs):
        copies.append(
            [
                pltpu.make_async_copy(
                    source(pair),
                    fields.at[:, pl.ds(4 + 2 * pair, 2), pl.ds(2, run)],
                    in_sem.at[pair],
                )
            ]
        )
        if final:
            copies[-1].append(
                pltpu.make_async_copy(
                    anchor.at[:, pl.ds(2 * pair, 2)],
                    base.at[:, pl.ds(2 + 2 * pair, 2)],
                    q_sem.at[pair],
                )
            )
        for copy in copies[-1]:
            copy.start()
    sweep = Sweep(
        fields, middle, coeffs, slopes, flow, result, base, factors, lambda step: layers
    )

    def prepare(pair):
        for copy in copies[pair]:
            copy.wait()
        for p in range(2):
            close_planes(fields, 4 + 2 * pair + p)

    flow_copy.wait()
    for pair in range(4):
        prepare(pair)

    def begin(step, carry):
        sweep.fill(step)
        sweep.first_slopes(step)
        sweep.first(step)
        sweep.mask_first(step)
        return carry

    lax.fori_loop(2, 4, begin, 0)
    for pair in range(4, pairs):
        prepare(pair)
    begin(4, 0)

    def body(step, carry):
        sweep.fill(step + 3)
        sweep.last_slopes(step)
        sweep.first_slopes(step + 3)
        sweep.last(step)
        sweep.first(step + 3)
        sweep.mask_last(step)
        sweep.mask_first(step + 3)
        return carry

    lax.fori_loop(2, pairs - 3, body, 0)
    pushes = [
        pltpu.make_async_copy(
            middle.at[:, pl.ds(4 + 8 * end, 4)], edges.at[:, pl.ds(4 * end, 4)], out_sem.at[end]
        )
        for end in range(2)
    ]
    for push in pushes:
        push.start()
    sweep.last_slopes(pairs - 3)
    sweep.last(pairs - 3)
    sweep.mask_last(pairs - 3)
    pushes.append(pltpu.make_async_copy(result, out, out_sem.at[2]))
    pushes[-1].start()
    for push in pushes:
        push.wait()


def outer_kernel(factors, final, *refs):
    state, edges, low, high, flow_in, below, above = refs[:7]
    if final:
        anchor, q_low, q_high, part, out = refs[7:12]
        scratch = refs[12:]
        base, q_sem, part_sem = scratch[-3:]
    else:
        out, send_low, send_high = refs[7:10]
        scratch = refs[10:]
        base = None
    fields, middle, coeffs, result, slopes, flow, in_sem, out_sem, flow_sem = scratch[:9]
    run = coeffs.shape[2]
    levels = flow_in.shape[1]
    height = fields.shape[1] - 2 * layers
    rows = run * 8
    lower, upper = edge("wa")
    flow_copy = pltpu.make_async_copy(flow_in, flow.at[:, pl.ds(1, levels)], flow_sem)
    flow_copy.start()
    far = state.shape[1] - 4

    def fetch(half):
        copies = [
            pltpu.make_async_copy(
                state.at[:, pl.ds(far * half, 4)],
                fields.at[:, pl.ds(4 + 12 * half, 4), pl.ds(2, run)],
                in_sem.at[half],
            ),
            pltpu.make_async_copy(
                edges.at[:, pl.ds(4 * half, 4)],
                middle.at[:, pl.ds(4 + 8 * half, 4)],
                in_sem.at[2 + half],
            ),
        ]
        if final:
            copies.append(
                pltpu.make_async_copy(
                    anchor.at[:, pl.ds(12 * half, 4)],
                    base.at[:, pl.ds(2 + 12 * half, 4)],
                    q_sem.at[half],
                )
            )
        return copies

    for half in range(2):
        for copy in fetch(half):
            copy.start()
    if final:
        part_copy = pltpu.make_async_copy(part, result, part_sem)
        part_copy.start()

    def layer(ref, f, z):
        value = ref[pl.ds((f * layers + z) * rows, rows), :].astype(f32)
        return [value[8 * i : 8 * i + 8] for i in range(run)]

    for f in range(4):
        for z in range(layers):
            put_plane(fields, f, z, layer(low, f, z))
            put_plane(fields, f, layers + height + z, layer(high, f, z))
        if final:
            for z in range(2):
                for target, ref, from_z in ((z, q_low, layers - 2 + z), (height + 2 + z, q_high, z)):
                    for i, value in enumerate(layer(ref, f, from_z)):
                        base[f, target, i] = value
    flow_copy.wait()
    half_run = run // 2
    for f in range(4):
        at = pl.ds(f * half_run * 8, half_run * 8)
        under, over, over_next = (below[at, :], above[0, at, :], above[1, at, :])
        for j in range(half_run):
            piece = slice(8 * j, 8 * j + 8)
            values = (
                under[piece].astype(f32),
                jnp.where(upper, flow[f, levels, j], over[piece].astype(f32)),
                over_next[piece].astype(f32),
            )
            for level, value in zip((0, levels + 1, levels + 2), values):
                flow[f, level, j] = value
                if j == 0:
                    flow[f, level, half_run] = down(value)
    if final:
        part_copy.wait()
    sweep = Sweep(
        fields, middle, coeffs, slopes, flow, result, base, factors, lambda step: 8 * (step // 4)
    )

    def push(half):
        planes = pl.ds(4 * half, 4)
        return pltpu.make_async_copy(result.at[:, planes], out.at[:, planes], out_sem.at[half])

    def body(half, carry):
        for copy in fetch(half):
            copy.wait()
        for p in range(4):
            close_planes(fields, 4 + 12 * half + p)
        for k in range(2):
            sweep.first_slopes(8 * half + k, k)
        for k in range(3):
            sweep.fill(7 * half + k)
        for k in range(2):
            sweep.first(8 * half + k, k)
        for k in range(2):
            sweep.mask_first(8 * half + k)

        @pl.when(lower & (half == 0))
        def _():
            sweep.clear_first(0)

        @pl.when(upper & (half == 1))
        def _():
            sweep.clear_first(9)

        for k in range(2):
            sweep.last_slopes(6 * half + k, 2 + k)
        for k in range(2):
            sweep.last(6 * half + k, 2 + k)
        for k in range(2):
            sweep.mask_last(6 * half + k)
        if not final:
            push(half).start()
        return carry

    lax.fori_loop(0, 2, body, 0)
    if final:
        pushes = []
        for s in range(8):
            inner, outer = run_rows(s, run, height)
            pushes.append(
                pltpu.make_async_copy(result.at[:, s, inner], out.at[:, outer], out_sem.at[s])
            )
        for copy in pushes:
            copy.start()
        for copy in pushes:
            copy.wait()
    else:
        cast_layers(result, send_low, send_high)
        for half in range(2):
            push(half).wait()


def advance(height, run, halo, flow, factors, state=None, parts=None, anchor=None, anchor_halo=None):
    final = anchor is not None
    flow, below, above = flow
    pairs = height // 2
    natural = (4, 8, run * height + pad, 128)
    half_block = (4, height // 2, run, 8, 128)
    inner_result = natural if final else half_block
    common = [
        pltpu.VMEM((4, height + 2 * layers, run + 4, 8, 128), f32),
        pltpu.VMEM((4, height + 4, run + 4, 8, 128), f32),
        pltpu.VMEM((4, height + 4, run, 8, 128), f32),
        pltpu.VMEM(inner_result, f32),
        pltpu.VMEM((4, 4, 2, run, 8, 128), f32),
        pltpu.VMEM((4, flow.shape[1] + 3, run // 2 + 1, 8, 128), f32),
    ]
    sems = [
        pltpu.SemaphoreType.DMA((pairs,)),
        pltpu.SemaphoreType.DMA((8,)),
        pltpu.SemaphoreType.DMA,
    ]
    base = pltpu.VMEM((4, height + 4, run, 8, 128), f32)
    edges_shape = shape_of(4, 8, run + 4, 8, 128)
    operands = [*parts, flow, anchor] if final else [state, flow]
    inner, edges = call(
        functools.partial(inner_kernel, factors, final),
        [shape_of(*inner_result), edges_shape],
        [hbm] * len(operands),
        [hbm, hbm],
        common + sems + ([base, pltpu.SemaphoreType.DMA((pairs,))] if final else []),
    )(*operands)
    operands = [parts[1] if final else state, edges, *halo, flow, below, above]
    in_specs = [hbm, hbm, vmem, vmem, hbm, vmem, vmem]
    if final:
        (out,) = call(
            functools.partial(outer_kernel, factors, final),
            [shape_of(4, (run * 8 - 2 * reach) * height, 128)],
            in_specs + [hbm, vmem, vmem, hbm],
            [hbm],
            common + sems + [base, pltpu.SemaphoreType.DMA((2,)), pltpu.SemaphoreType.DMA],
        )(*operands, anchor, *anchor_halo, inner)
        return out
    layer = shape_of(4 * layers * run * 8, 128, dtype=bf16)
    outer, send_low, send_high = call(
        functools.partial(outer_kernel, factors, final),
        [shape_of(*half_block), layer, layer],
        in_specs,
        [hbm, vmem, vmem],
        common + sems,
    )(*operands)
    return ((inner, outer), send_low, send_high)


def neighbours(axis, forward):
    count = lax.axis_size(axis)
    return [(i, i + 1) if forward else (i + 1, i) for i in range(count - 1)]


def exchange(to_next, to_previous, axis):
    return (
        lax.ppermute(to_next, axis, neighbours(axis, True)),
        lax.ppermute(to_previous, axis, neighbours(axis, False)),
    )


def to_owners(pieces):
    devices = len(pieces)
    moved = [pieces[0]]
    for shift in range(1, devices):
        ring = [(i, (i + shift) % devices) for i in range(devices)]
        moved.append(lax.ppermute(pieces[shift], "wa", ring))
    return moved


def shards(les_flow, y_index, y_weight, acoustic_state):
    devices = lax.axis_size("wa")
    _, columns, levels, width = les_flow.shape
    cut, first, last = cut_tiles(les_flow, acoustic_state, devices)
    tiles = to_owners(cut)
    before, after = exchange(last, first, "gx")
    skip = 4 * reach * acoustic_state.shape[2]
    tails = cut_tails(before, after, skip, levels, devices)
    before, after, *tails = lax.optimization_barrier((before, after, *tails))
    state, send_low, send_high = widen(acoustic_state, before, after)
    send_low, send_high, *late = lax.optimization_barrier((send_low, send_high, *tails[3:]))
    tails = to_owners(tails[:3] + late)
    tiles, tails, send_low, send_high = lax.optimization_barrier(
        (tiles, tails, send_low, send_high)
    )
    halo = exchange(send_high, send_low, "wa")
    flow, low, high = spread(
        tiles, tails, y_index, y_weight, columns, levels // devices, width
    )
    below, above = exchange(high, low, "wa")
    flow = (flow, below, above)
    height, run = state.shape[1:3]
    parts, send_low, send_high = advance(height, run, halo, flow, (1 / 4, 1 / 3), state=state)
    half_halo = exchange(send_high, send_low, "wa")
    result = advance(
        height, run, half_halo, flow, (1 / 2, 1.0), parts=parts, anchor=state, anchor_halo=halo
    )
    return result.reshape(acoustic_state.shape)


def solution(mesh):
    placed = (P(None, "gx", None, "wa"), P(), P(), P(None, "gx", "wa", None))
    return jax.shard_map(
        shards, mesh=mesh, in_specs=placed, out_specs=P(None, "gx", "wa", None), check_vma=False
    )
```

```python
import functools

import jax
import jax.numpy as jnp
from jax import lax
from jax.experimental import pallas as pl
from jax.experimental.pallas import tpu as pltpu
from jax.sharding import PartitionSpec as P

time_step = 0.4
unit = time_step / 12.0
reach = 8
ahead = 4
layers = 4
pad = 8
group = 3
f32 = jnp.float32
bf16 = jnp.bfloat16
grant = 60 * 2**20
vmem = pl.BlockSpec(memory_space=pltpu.VMEM)
hbm = pl.BlockSpec(memory_space=pl.ANY)


def shape_of(*dims, dtype=f32):
    return jax.ShapeDtypeStruct(dims, dtype)


def call(kernel, out_shape, in_specs, out_specs, scratch=()):
    return pl.pallas_call(
        kernel,
        out_shape=out_shape,
        in_specs=in_specs,
        out_specs=out_specs,
        scratch_shapes=list(scratch),
        compiler_params=pltpu.CompilerParams(vmem_limit_bytes=grant),
    )


def edge(axis):
    me = lax.axis_index(axis)
    return (me == 0, me == lax.axis_size(axis) - 1)


def up(value):
    return pltpu.roll(value, 1, 0)


def down(value):
    return pltpu.roll(value, 7, 0)


def side_by_side(les, pair, column):
    return jnp.concatenate(
        [les[2 * pair, column].astype(f32), les[2 * pair + 1, column].astype(f32)], axis=1
    )


def cut_kernel(les, state, *refs):
    *tiles, first, last, wide, ends, sem = refs
    devices = len(tiles)
    columns, levels, width = les.shape[1:]
    own = levels // devices
    me = lax.axis_index("wa")
    starts = (0, state.shape[1] - reach)
    copies = [
        pltpu.make_async_copy(state.at[:, pl.ds(starts[end], reach)], ends.at[end], sem.at[end])
        for end in range(2)
    ]
    for copy in copies:
        copy.start()

    def body(column, carry):
        for pair in range(2):
            wide[pair, column] = jnp.concatenate(
                [les[2 * pair, column].astype(f32), les[2 * pair + 1, column].astype(f32)], axis=1
            )
        return carry

    lax.fori_loop(0, columns, body, 0, unroll=8)
    for shift in range(devices):
        row = pl.multiple_of(lax.rem(me + shift, devices) * own, own)
        tiles[shift][...] = (
            wide[:, :, pl.ds(row, own), :].reshape(2 * columns * own, 2 * width).astype(bf16)
        )
    rows = 4 * reach * state.shape[2]
    les_rows = 2 * ahead * levels
    for end, (target, start) in enumerate(((first, 0), (last, columns - ahead))):
        copies[end].wait()
        target[pl.ds(0, rows), :] = ends[end].reshape(rows, 128).astype(bf16)
        target[pl.ds(rows, les_rows), :] = (
            wide[:, start : start + ahead].reshape(les_rows, 128).astype(bf16)
        )


def cut_tiles(les_flow, state, devices):
    _, columns, levels, width = les_flow.shape
    tile = shape_of(2 * columns * (levels // devices), 2 * width, dtype=bf16)
    end = shape_of(4 * reach * state.shape[2] + 2 * ahead * levels, 128, dtype=bf16)
    *tiles, first, last = call(
        cut_kernel,
        [tile] * devices + [end] * 2,
        [vmem, hbm],
        [vmem] * (devices + 2),
        [
            pltpu.VMEM((2, columns, levels, 2 * width), f32),
            pltpu.VMEM((2, 4, reach, state.shape[2], 128), f32),
            pltpu.SemaphoreType.DMA((2,)),
        ],
    )(les_flow, state)
    return (tiles, first, last)


def tails_kernel(skip, levels, before, after, *refs):
    tails, wide = (refs[:-1], refs[-1])
    devices = len(tails)
    own = levels // devices
    rows = 2 * ahead * levels
    wide[0] = before[pl.ds(skip, rows), :].astype(f32).reshape(2, ahead, levels, 128)
    wide[1] = after[pl.ds(skip, rows), :].astype(f32).reshape(2, ahead, levels, 128)
    me = lax.axis_index("wa")
    for shift in range(devices):
        row = pl.multiple_of(lax.rem(me + shift, devices) * own, own)
        tails[shift][...] = (
            wide[:, :, :, pl.ds(row, own), :].reshape(4 * ahead * own, 128).astype(bf16)
        )


def cut_tails(before, after, skip, levels, devices):
    tail = shape_of(4 * ahead * (levels // devices), 128, dtype=bf16)
    return call(
        functools.partial(tails_kernel, skip, levels),
        [tail] * devices,
        [vmem, vmem],
        [vmem] * devices,
        [pltpu.VMEM((2, 2, ahead, levels, 128), f32)],
    )(before, after)


def run_rows(s, run, height):
    first = max(0, reach - run * s)
    count = min(run, 8 * run - reach - run * s) - first
    inner = pl.ds(first * height, count * height)
    return (inner, pl.ds((run * s + first - reach) * height, count * height))


def widen_kernel(state, before, after, out, send_low, send_high, whole, result, sem, out_sem):
    height, run = out.shape[1:3]
    pitch = run * height + pad
    flat_whole = whole.reshape(32 * pitch, 128)
    fetches = []
    for f in range(4):
        for s in range(8):
            inner, outer = run_rows(s, run, height)
            fetches.append(
                pltpu.make_async_copy(state.at[f, outer], whole.at[f, s, inner], sem.at[f, s])
            )
    for fetch in fetches:
        fetch.start()
    rows = reach * height
    for f in range(4):
        part = pl.ds(f * rows, rows)
        whole[f, 0, pl.ds(0, rows), :] = before[part, :].astype(f32)
        whole[f, 7, pl.ds(run * height - rows, rows), :] = after[part, :].astype(f32)
    pushes = []
    for f in range(4):
        for s in range(8):
            fetches[8 * f + s].wait()

        def body(step, carry, f=f):
            for p in range(4):
                for i in range(run):
                    start = f * 8 * pitch + i * height + 4 * step + p
                    result[f, 4 * step + p, i] = flat_whole[pl.ds(start, 8, stride=pitch), :]
            return carry

        lax.fori_loop(0, height // 4, body, 0)
        push = pltpu.make_async_copy(result.at[f], out.at[f], out_sem.at[f])
        push.start()
        pushes.append(push)
    cast_layers(result, send_low, send_high)
    for push in pushes:
        push.wait()


def cast_layers(result, send_low, send_high):
    _, height, run = result.shape[:3]
    rows = run * 8
    for f in range(4):
        for z in range(layers):
            at = pl.ds((f * layers + z) * rows, rows)
            send_low[at, :] = result[f, z].reshape(rows, 128).astype(bf16)
            send_high[at, :] = result[f, height - layers + z].reshape(rows, 128).astype(bf16)


def widen(state, before, after):
    columns, height = state.shape[1:3]
    run = (columns + 2 * reach) // 8
    layer = shape_of(4 * layers * run * 8, 128, dtype=bf16)
    return call(
        widen_kernel,
        [shape_of(4, height, run, 8, 128), layer, layer],
        [hbm, vmem, vmem],
        [hbm, vmem, vmem],
        [
            pltpu.VMEM((4, 8, run * height + pad, 128), f32),
            pltpu.VMEM((4, height, run, 8, 128), f32),
            pltpu.SemaphoreType.DMA((4, 8)),
            pltpu.SemaphoreType.DMA((4,)),
        ],
    )(state.reshape(4, columns * height, 128), before, after)


def spread_kernel(devices, width, *refs):
    tiles, tails = (refs[:devices], refs[devices : 2 * devices])
    y_index, y_weight, out, send_low, send_high, wide = refs[2 * devices :]
    me = lax.axis_index("wa")
    left_weight = (1.0 - y_weight[...].astype(f32)).astype(bf16).astype(f32)
    right_weight = y_weight[...].astype(f32)
    row_ids = lax.broadcasted_iota(jnp.int32, (width, 128), 0)
    nothing = jnp.zeros((width, 128), f32)
    total, tail = (None, None)
    for shift in range(devices):
        first_row = lax.rem(me - shift + devices, devices) * width
        gap = y_index[...] - first_row - row_ids
        matrix = jnp.where(gap == 0, left_weight, 0.0) + jnp.where(gap == -1, right_weight, 0.0)
        pair = jnp.concatenate(
            [
                jnp.concatenate([matrix, nothing], axis=1),
                jnp.concatenate([nothing, matrix], axis=1),
            ],
            axis=0,
        ).astype(bf16)
        part = jnp.dot(tiles[shift][...], pair, preferred_element_type=f32)
        tail_part = jnp.dot(tails[shift][...], pair, preferred_element_type=f32)
        total = part if total is None else total + part
        tail = tail_part if tail is None else tail + tail_part
    levels, run = (out.shape[1], out.shape[2] - 1)
    columns = total.shape[0] // (2 * levels)
    wide_columns = columns + 2 * ahead
    _, is_end = edge("gx")
    for f in range(4):
        pair, lanes = (f // 2, slice(128 * (f % 2), 128 * (f % 2 + 1)))
        main = total[pair * columns * levels : (pair + 1) * columns * levels, lanes]
        side = ahead * levels
        left = tail[pair * side : (pair + 1) * side, lanes]
        right = tail[(2 + pair) * side : (3 + pair) * side, lanes]
        right = jnp.where(is_end, jnp.concatenate([main[-levels:]] * ahead, axis=0), right)
        wide[pl.ds(f * wide_columns * levels, wide_columns * levels), :] = jnp.concatenate(
            [left, main, right], axis=0
        )
    for f in range(4):

        def body(k, carry, f=f):
            for j in range(run):
                start = (f * wide_columns + j) * levels + k
                value = wide[pl.ds(start, 8, stride=run * levels), :]
                out[f, k, j] = value
                if j == 0:
                    out[f, k, run] = down(value)
            return carry

        lax.fori_loop(0, levels, body, 0)
        rows = run * 8
        send_high[pl.ds(f * rows, rows), :] = (
            out[f, levels - 1, :run].reshape(rows, 128).astype(bf16)
        )
        for k in range(2):
            send_low[pl.ds((4 * k + f) * rows, rows), :] = (
                out[f, k, :run].reshape(rows, 128).astype(bf16)
            )


def spread(tiles, tails, y_index, y_weight, columns, levels, width):
    devices = len(tiles)
    run = (columns + 2 * ahead) // 8
    return call(
        functools.partial(spread_kernel, devices, width),
        [
            shape_of(4, levels, run + 1, 8, 128),
            shape_of(2 * 4 * run * 8, 128, dtype=bf16),
            shape_of(4 * run * 8, 128, dtype=bf16),
        ],
        [vmem] * (2 * devices + 2),
        [vmem] * 3,
        [pltpu.VMEM((4 * (columns + 2 * ahead) * levels, 128), f32)],
    )(*tiles, *tails, y_index.reshape(1, 128), y_weight.reshape(1, 128))


def band_matrix():
    row, column = [lax.broadcasted_iota(jnp.int32, (256, 256), axis) for axis in range(2)]
    gap = jnp.where((row < 128) == (column < 128), row - column, 128)
    near = jnp.where(gap == 1, 8.0, jnp.where(gap == -1, -8.0, 0.0))
    return (near + jnp.where(gap == 2, -1.0, jnp.where(gap == -2, 1.0, 0.0))).astype(bf16)


def difference(low_far, low, high, high_far):
    return 8.0 * (high - low) - (high_far - low_far)


def spanwise(source, plane, slopes, band):
    run = source.shape[2] - 4
    for pair in range(2):
        sides = [
            source[f, pl.ds(plane, 2), pl.ds(2, run)].reshape(2 * run * 8, 128).astype(bf16)
            for f in (2 * pair, 2 * pair + 1)
        ]
        both = jnp.dot(jnp.concatenate(sides, axis=1), band, preferred_element_type=f32)
        slopes[2 * pair] = both[:, :128].reshape(2, run, 8, 128)
        slopes[2 * pair + 1] = both[:, 128:].reshape(2, run, 8, 128)


def stage(source, plane, coeffs, across, anchor, store, slopes_y, factor):
    run = coeffs.shape[2]
    places = [(p, u) for p in range(2) for u in range(group)]
    for first in range(0, run, group):
        speeds = {
            (f, p, u): coeffs[f, across + p, first + u] for f in range(3) for p, u in places
        }
        rates, spreads, own_rates, centers = ({}, {}, {}, {})
        for f in range(4):
            line = {
                (p, u): source[f, plane + p, first + u + 2]
                for p in range(2)
                for u in range(-2, group + 2)
            }
            for u in range(group):
                for p in (-2, -1, 2, 3):
                    line[p, u] = source[f, plane + p, first + u + 2]
            for p, u in places:
                slope_x = difference(*[line[p, u + k] for k in (-2, -1, 1, 2)])
                slope_z = difference(*[line[p + k, u] for k in (-2, -1, 1, 2)])
                slope_y = slopes_y[f, p, first + u]
                rate = (
                    speeds[0, p, u] * slope_x + speeds[1, p, u] * slope_y + speeds[2, p, u] * slope_z
                )
                if f == 0:
                    own_rates[p, u] = rate
                    centers[p, u] = line[p, u]
                    for k, slope in enumerate((slope_x, slope_y, slope_z)):
                        rates[k + 1, p, u] = unit * slope
                else:
                    rate += rates[f, p, u]
                    start = line[p, u] if anchor is None else anchor(f, p, first + u)
                    store(f, p, first + u, start - factor * rate)
                    slope = (slope_x, slope_y, slope_z)[f - 1]
                    spreads[p, u] = slope if f == 1 else spreads[p, u] + slope
        for p, u in places:
            rate = own_rates[p, u] + coeffs[3, across + p, first + u] * spreads[p, u]
            start = centers[p, u] if anchor is None else anchor(0, p, first + u)
            store(0, p, first + u, start - factor * rate)


def fill_coeffs(flow, level, coeffs, plane):
    run = coeffs.shape[2]
    for f in range(4):
        here = [flow[f, level, j] for j in range(run // 2 + 1)]
        above = [flow[f, level + 1, j] for j in range(run // 2 + 1)]
        middle = [0.5 * (a + b) for a, b in zip(here, above)]
        for p, line in enumerate((here, middle)):
            for i in range(run):
                j = i // 2
                value = line[j] if i % 2 == 0 else 0.5 * (line[j] + line[j + 1])
                if f < 3:
                    value = (0.3 * unit) * value
                else:
                    speed = 1.0 + 0.2 * value
                    value = unit * (speed * speed)
                coeffs[f, plane + p, i] = value


def put_plane(target, f, plane, values):
    run = len(values)
    for i, value in enumerate(values):
        target[f, plane, i + 2] = value
    for i in range(2):
        target[f, plane, i] = up(values[run - 2 + i])
        target[f, plane, run + 2 + i] = down(values[i])


def close_planes(target, plane):
    run = target.shape[2] - 4
    for f in range(4):
        for i in range(2):
            target[f, plane, i] = up(target[f, plane, run + i])
            target[f, plane, run + 2 + i] = down(target[f, plane, 2 + i])


def mask_columns(target, planes, offset, left, right):
    run = target.shape[2] - 2 * offset
    sublane = lax.broadcasted_iota(jnp.int32, (8, 128), 0)

    @pl.when(left)
    def _():
        for f in range(4):
            for plane in planes:
                for i in range(reach):
                    value = target[f, plane, offset + i]
                    target[f, plane, offset + i] = jnp.where(sublane == 0, 0.0, value)

    @pl.when(right)
    def _():
        for f in range(4):
            for plane in planes:
                for i in range(run - reach, run):
                    value = target[f, plane, offset + i]
                    target[f, plane, offset + i] = jnp.where(sublane == 7, 0.0, value)


class Sweep:
    def __init__(self, fields, middle, coeffs, slopes, flow, result, base, factors, shift):
        self.fields, self.middle, self.coeffs, self.slopes = (fields, middle, coeffs, slopes)
        self.flow, self.result, self.base, self.factors = (flow, result, base, factors)
        self.shift = shift
        self.run = coeffs.shape[2]
        self.band = band_matrix()
        self.left, self.right = edge("gx")

    def fill(self, step):
        fill_coeffs(self.flow, step, self.coeffs, 2 * step)

    def first_slopes(self, step, slot=0):
        spanwise(self.fields, 2 * step + 2, self.slopes.at[slot], self.band)

    def first(self, step, slot=0):
        run, middle, base = (self.run, self.middle, self.base)

        def store(f, p, i, value):
            plane = 2 * step + p
            middle[f, plane, i + 2] = value
            if i < 2:
                middle[f, plane, run + 2 + i] = down(value)
            if i >= run - 2:
                middle[f, plane, i - (run - 2)] = up(value)

        anchor = None
        if base is not None:

            def anchor(f, p, i):
                return base[f, 2 * step + p, i]

        stage(
            self.fields, 2 * step + 2, self.coeffs, 2 * step, anchor, store,
            self.slopes.at[slot], self.factors[0],
        )

    def mask_first(self, step):
        mask_columns(self.middle, [2 * step, 2 * step + 1], 2, self.left, self.right)

    def clear_first(self, step):
        for f in range(4):
            for p in range(2):
                for i in range(self.run + 4):
                    self.middle[f, 2 * step + p, i] = jnp.zeros((8, 128), f32)

    def last_slopes(self, step, slot=2):
        spanwise(self.middle, 2 * step + 2, self.slopes.at[slot], self.band)

    def last(self, step, slot=2):
        run, result = (self.run, self.result)

        def anchor(f, p, i):
            if self.base is not None:
                return self.base[f, 2 * step + 2 + p, i]
            return self.fields[f, 2 * step + 4 + p, i + 2]

        def store(f, p, i, value):
            z = 2 * step + p
            if self.base is None:
                result[f, z - self.shift(step), i] = value
            else:
                pitch = result.shape[2]
                height = (pitch - pad) // run
                flat_result = result.reshape(32 * pitch, 128)
                flat_result[pl.ds(f * 8 * pitch + i * height + z, 8, stride=pitch), :] = value

        stage(
            self.middle, 2 * step + 2, self.coeffs, 2 * step + 2, anchor, store,
            self.slopes.at[slot], self.factors[1],
        )

    def mask_last(self, step):
        if self.base is None:
            first = 2 * step - self.shift(step)
            mask_columns(self.result, [first, first + 1], 0, self.left, self.right)


def inner_kernel(factors, final, *refs):
    if final:
        inner, outer, flow_in, anchor, out, edges = refs[:6]
        scratch = refs[6:]
        base, q_sem = scratch[-2:]
    else:
        state, flow_in, out, edges = refs[:4]
        scratch = refs[4:]
        base = None
    fields, middle, coeffs, result, slopes, flow, in_sem, out_sem, flow_sem = scratch[:9]
    run = coeffs.shape[2]
    levels = flow_in.shape[1]
    pairs = in_sem.shape[0]

    def source(pair):
        if not final:
            return state.at[:, pl.ds(2 * pair, 2)]
        if pair < 2:
            return outer.at[:, pl.ds(2 * pair, 2)]
        if pair >= pairs - 2:
            return outer.at[:, pl.ds(2 * (pair - (pairs - 4)), 2)]
        return inner.at[:, pl.ds(2 * (pair - 2), 2)]

    flow_copy = pltpu.make_async_copy(flow_in, flow.at[:, pl.ds(1, levels)], flow_sem)
    flow_copy.start()
    copies = []
    for pair in range(pairs):
        copies.append(
            [
                pltpu.make_async_copy(
                    source(pair),
                    fields.at[:, pl.ds(4 + 2 * pair, 2), pl.ds(2, run)],
                    in_sem.at[pair],
                )
            ]
        )
        if final:
            copies[-1].append(
                pltpu.make_async_copy(
                    anchor.at[:, pl.ds(2 * pair, 2)],
                    base.at[:, pl.ds(2 + 2 * pair, 2)],
                    q_sem.at[pair],
                )
            )
        for copy in copies[-1]:
            copy.start()
    sweep = Sweep(
        fields, middle, coeffs, slopes, flow, result, base, factors, lambda step: layers
    )

    def prepare(pair):
        for copy in copies[pair]:
            copy.wait()
        for p in range(2):
            close_planes(fields, 4 + 2 * pair + p)

    flow_copy.wait()
    for pair in range(4):
        prepare(pair)

    def begin(step, carry):
        sweep.fill(step)
        sweep.first_slopes(step)
        sweep.first(step)
        sweep.mask_first(step)
        return carry

    lax.fori_loop(2, 4, begin, 0)
    for pair in range(4, pairs):
        prepare(pair)
    begin(4, 0)

    def body(step, carry):
        sweep.fill(step + 3)
        sweep.last_slopes(step)
        sweep.first_slopes(step + 3)
        sweep.last(step)
        sweep.first(step + 3)
        sweep.mask_last(step)
        sweep.mask_first(step + 3)
        return carry

    lax.fori_loop(2, pairs - 3, body, 0)
    pushes = [
        pltpu.make_async_copy(
            middle.at[:, pl.ds(4 + 8 * end, 4)], edges.at[:, pl.ds(4 * end, 4)], out_sem.at[end]
        )
        for end in range(2)
    ]
    for push in pushes:
        push.start()
    sweep.last_slopes(pairs - 3)
    sweep.last(pairs - 3)
    sweep.mask_last(pairs - 3)
    pushes.append(pltpu.make_async_copy(result, out, out_sem.at[2]))
    pushes[-1].start()
    for push in pushes:
        push.wait()


def outer_kernel(factors, final, *refs):
    state, edges, low_in, high_in, flow_in, below_in, above_in = refs[:7]
    if final:
        anchor, q_low_in, q_high_in, part, out = refs[7:12]
        scratch = refs[12:]
        base, q_sem, part_sem = scratch[-3:]
        halos_in = (low_in, high_in, q_low_in, q_high_in, below_in, above_in)
    else:
        out, send_low, send_high = refs[7:10]
        scratch = refs[10:]
        base = None
        halos_in = (low_in, high_in, below_in, above_in)
    fields, middle, coeffs, result, slopes, flow, in_sem, out_sem, flow_sem, halos, halo_sem = (
        scratch[:11]
    )
    halo_copies = [
        pltpu.make_async_copy(ref, halos.at[index, pl.ds(0, ref.shape[0])], halo_sem.at[index])
        for index, ref in enumerate(halos_in)
    ]
    for copy in halo_copies:
        copy.start()
    run = coeffs.shape[2]
    levels = flow_in.shape[1]
    height = fields.shape[1] - 2 * layers
    rows = run * 8
    lower, upper = edge("wa")
    flow_copy = pltpu.make_async_copy(flow_in, flow.at[:, pl.ds(1, levels)], flow_sem)
    flow_copy.start()
    far = state.shape[1] - 4

    def fetch(half):
        copies = [
            pltpu.make_async_copy(
                state.at[:, pl.ds(far * half, 4)],
                fields.at[:, pl.ds(4 + 12 * half, 4), pl.ds(2, run)],
                in_sem.at[half],
            ),
            pltpu.make_async_copy(
                edges.at[:, pl.ds(4 * half, 4)],
                middle.at[:, pl.ds(4 + 8 * half, 4)],
                in_sem.at[2 + half],
            ),
        ]
        if final:
            copies.append(
                pltpu.make_async_copy(
                    anchor.at[:, pl.ds(12 * half, 4)],
                    base.at[:, pl.ds(2 + 12 * half, 4)],
                    q_sem.at[half],
                )
            )
        return copies

    for half in range(2):
        for copy in fetch(half):
            copy.start()
    if final:
        part_copy = pltpu.make_async_copy(part, result, part_sem)
        part_copy.start()

    for copy in halo_copies:
        copy.wait()

    def layer(index, f, z):
        value = halos[index, pl.ds((f * layers + z) * rows, rows), :].astype(f32)
        return [value[8 * i : 8 * i + 8] for i in range(run)]

    for f in range(4):
        for z in range(layers):
            put_plane(fields, f, z, layer(0, f, z))
            put_plane(fields, f, layers + height + z, layer(1, f, z))
        if final:
            for z in range(2):
                for target, index, from_z in ((z, 2, layers - 2 + z), (height + 2 + z, 3, z)):
                    for i, value in enumerate(layer(index, f, from_z)):
                        base[f, target, i] = value
    flow_copy.wait()
    half_run = run // 2
    for f in range(4):
        flow_rows = half_run * 8
        under, over, over_next = [
            halos[
                len(halos_in) - 2 + side,
                pl.ds((4 * k + f) * flow_rows, flow_rows),
                :,
            ]
            for side, k in ((0, 0), (1, 0), (1, 1))
        ]
        for j in range(half_run):
            piece = slice(8 * j, 8 * j + 8)
            values = (
                under[piece].astype(f32),
                jnp.where(upper, flow[f, levels, j], over[piece].astype(f32)),
                over_next[piece].astype(f32),
            )
            for level, value in zip((0, levels + 1, levels + 2), values):
                flow[f, level, j] = value
                if j == 0:
                    flow[f, level, half_run] = down(value)
    sweep = Sweep(
        fields, middle, coeffs, slopes, flow, result, base, factors, lambda step: 8 * (step // 4)
    )

    def push(half):
        planes = pl.ds(4 * half, 4)
        return pltpu.make_async_copy(result.at[:, planes], out.at[:, planes], out_sem.at[half])

    def body(half, carry):
        for copy in fetch(half):
            copy.wait()
        for p in range(4):
            close_planes(fields, 4 + 12 * half + p)
        for k in range(2):
            sweep.first_slopes(8 * half + k, k)
        for k in range(3):
            sweep.fill(7 * half + k)
        for k in range(2):
            sweep.first(8 * half + k, k)
        for k in range(2):
            sweep.mask_first(8 * half + k)

        @pl.when(lower & (half == 0))
        def _():
            sweep.clear_first(0)

        @pl.when(upper & (half == 1))
        def _():
            sweep.clear_first(9)

        if final:

            @pl.when(half == 0)
            def _():
                part_copy.wait()

        for k in range(2):
            sweep.last_slopes(6 * half + k, 2 + k)
        for k in range(2):
            sweep.last(6 * half + k, 2 + k)
        for k in range(2):
            sweep.mask_last(6 * half + k)
        if not final:
            push(half).start()
        return carry

    lax.fori_loop(0, 2, body, 0)
    if final:
        pushes = []
        for s in range(8):
            inner, outer = run_rows(s, run, height)
            pushes.append(
                pltpu.make_async_copy(result.at[:, s, inner], out.at[:, outer], out_sem.at[s])
            )
        for copy in pushes:
            copy.start()
        for copy in pushes:
            copy.wait()
    else:
        cast_layers(result, send_low, send_high)
        for half in range(2):
            push(half).wait()


def advance(height, run, halo, flow, factors, state=None, parts=None, anchor=None, anchor_halo=None):
    final = anchor is not None
    pairs = height // 2
    flow, *flow_halo = flow
    halo_scratch = [
        pltpu.VMEM((6 if final else 4, halo[0].shape[0], 128), bf16),
        pltpu.SemaphoreType.DMA((6,)),
    ]
    natural = (4, 8, run * height + pad, 128)
    half_block = (4, height // 2, run, 8, 128)
    inner_result = natural if final else half_block
    common = [
        pltpu.VMEM((4, height + 2 * layers, run + 4, 8, 128), f32),
        pltpu.VMEM((4, height + 4, run + 4, 8, 128), f32),
        pltpu.VMEM((4, height + 4, run, 8, 128), f32),
        pltpu.VMEM(inner_result, f32),
        pltpu.VMEM((4, 4, 2, run, 8, 128), f32),
        pltpu.VMEM((4, flow.shape[1] + 3, run // 2 + 1, 8, 128), f32),
    ]
    sems = [
        pltpu.SemaphoreType.DMA((pairs,)),
        pltpu.SemaphoreType.DMA((8,)),
        pltpu.SemaphoreType.DMA,
    ]
    base = pltpu.VMEM((4, height + 4, run, 8, 128), f32)
    edges_shape = shape_of(4, 8, run + 4, 8, 128)
    operands = [*parts, flow, anchor] if final else [state, flow]
    inner, edges = call(
        functools.partial(inner_kernel, factors, final),
        [shape_of(*inner_result), edges_shape],
        [hbm] * len(operands),
        [hbm, hbm],
        common + sems + ([base, pltpu.SemaphoreType.DMA((pairs,))] if final else []),
    )(*operands)
    operands = [parts[1] if final else state, edges, *halo, flow, *flow_halo]
    in_specs = [hbm] * 7
    if final:
        (out,) = call(
            functools.partial(outer_kernel, factors, final),
            [shape_of(4, (run * 8 - 2 * reach) * height, 128)],
            in_specs + [hbm] * 4,
            [hbm],
            common
            + sems
            + halo_scratch
            + [base, pltpu.SemaphoreType.DMA((2,)), pltpu.SemaphoreType.DMA],
        )(*operands, anchor, *anchor_halo, inner)
        return out
    layer = shape_of(4 * layers * run * 8, 128, dtype=bf16)
    outer, send_low, send_high = call(
        functools.partial(outer_kernel, factors, final),
        [shape_of(*half_block), layer, layer],
        in_specs,
        [hbm, vmem, vmem],
        common + sems + halo_scratch,
    )(*operands)
    return ((inner, outer), send_low, send_high)


def neighbours(axis, forward):
    count = lax.axis_size(axis)
    return [(i, i + 1) if forward else (i + 1, i) for i in range(count - 1)]


def exchange(to_next, to_previous, axis):
    return (
        lax.ppermute(to_next, axis, neighbours(axis, True)),
        lax.ppermute(to_previous, axis, neighbours(axis, False)),
    )


def to_owners(pieces):
    devices = len(pieces)
    moved = [pieces[0]]
    for shift in range(1, devices):
        ring = [(i, (i + shift) % devices) for i in range(devices)]
        moved.append(lax.ppermute(pieces[shift], "wa", ring))
    return moved


def shards(les_flow, y_index, y_weight, acoustic_state):
    devices = lax.axis_size("wa")
    _, columns, levels, width = les_flow.shape
    cut, first, last = cut_tiles(les_flow, acoustic_state, devices)
    tiles = to_owners(cut)
    before, after = exchange(last, first, "gx")
    skip = 4 * reach * acoustic_state.shape[2]
    tails = cut_tails(before, after, skip, levels, devices)
    before, after, *tails = lax.optimization_barrier((before, after, *tails))
    state, send_low, send_high = widen(acoustic_state, before, after)
    tiles[1], *late = lax.optimization_barrier((tiles[1], *tails[3:]))
    tails = to_owners(tails[:3] + late)
    tiles, tails, send_low, send_high = lax.optimization_barrier(
        (tiles, tails, send_low, send_high)
    )
    halo = exchange(send_high, send_low, "wa")
    flow, low, high = spread(
        tiles, tails, y_index, y_weight, columns, levels // devices, width
    )
    flow = (flow, *exchange(high, low, "wa"))
    height, run = state.shape[1:3]
    parts, send_low, send_high = advance(height, run, halo, flow, (1 / 4, 1 / 3), state=state)
    half_halo = exchange(send_high, send_low, "wa")
    result = advance(
        height, run, half_halo, flow, (1 / 2, 1.0), parts=parts, anchor=state, anchor_halo=halo
    )
    return result.reshape(acoustic_state.shape)


def solution(mesh):
    placed = (P(None, "gx", None, "wa"), P(), P(), P(None, "gx", "wa", None))
    return jax.shard_map(
        shards, mesh=mesh, in_specs=placed, out_specs=P(None, "gx", "wa", None), check_vma=False
    )
```
